32 devices in a mesh: table: 4 (over y, x), blk: 8 (over z, core).
Axes of the slice: x: 2, y: 2, z: 4, core: 2. Of those that a mesh axis runs over, the one named last changes fastest.
Arguments:
- cold_table: bfloat16 [131072, 128], P('table'), may hold values from -6 to 6
- slot_row: int32 [128, 2048], P(('table', 'blk')), may hold values from 0 to 32767
- slot_sample: int32 [128, 2048], P(('table', 'blk')), may hold values from 0 to 511
- slot_count: int32 [128, 2048], P(('table', 'blk')), may hold values from 0 to 15, as said below
- hot_table: bfloat16 [2048, 128], replicated, may hold values from -6 to 6
- hot_index: int32 [16384, 8], P(('table', 'blk')), may hold values from 0 to 2047
- hot_count: int32 [16384, 8], P(('table', 'blk')), may hold values from 1 to 15
- hot_cotangent: bfloat16 [16384, 128], P(('table', 'blk')), may hold values from -0.59765625 to 0.59765625
Outputs:
- features: bfloat16 [16384, 256], P(('table', 'blk'))
- hot_grad: float32 [2048, 128], P('blk')
The draws below stay inside these ranges and needn't reach their ends.
Inputs may be any that keep to these rules, and one draw needn't show every extreme that they name: `slot_count`: slots of a bucket that carry no request have count 0 and follow its used slots; in every draw, for every index of blk, one cold shard receives 2048 used slots from every device with that index.
All inputs are finite; a program needn't handle non-finite values.
Results may differ from the reference program's by a relative error of at most 0.001.
Values may be sent and summed in bfloat16 or wider, within the bound.
A program may use at most 128 MiB of HBM per device.

```python
import math
import jax
import jax.numpy as jnp
import numpy as np
from jax import lax

E = 128
S_DEV = 512
V_SHARD = 32768
KH = 8
CAP = 2048
PEERS = 4
REPLICAS = 8
BUCKETS = 128
SAMPLES = 16384
VROWS = 131072
HOT = 2048


def slot_law(key):
    base_key = jax.random.fold_in(key, 7)
    key_owner, key_load, key_row, key_sample, key_count = jax.random.split(base_key, 5)
    bucket = jnp.arange(BUCKETS, dtype=jnp.int32)
    source = bucket // PEERS
    owner = bucket % PEERS
    busiest = jax.random.randint(key_owner, (REPLICAS,), 0, PEERS)
    is_busy = busiest[source % REPLICAS] == owner
    loads = jax.random.randint(key_load, (BUCKETS,), CAP // 8, CAP // 2 + 1)
    used = jnp.where(is_busy, CAP, loads)
    live = jnp.arange(CAP, dtype=jnp.int32)[None, :] < used[:, None]
    rows_drawn = jax.random.randint(key_row, (BUCKETS, CAP), 0, V_SHARD)
    samples_drawn = jax.random.randint(key_sample, (BUCKETS, CAP), 0, S_DEV)
    counts_drawn = jnp.where(live, jax.random.randint(key_count, (BUCKETS, CAP), 1, 16), 0)
    return (rows_drawn, samples_drawn, counts_drawn)


def draw_slot_row(key, part):
    return slot_law(key)[0]


def draw_slot_sample(key, part):
    return slot_law(key)[1]


def draw_slot_count(key, part):
    return slot_law(key)[2]


def place_ends(entries, key, least, largest):
    place = [jax.random.randint(jax.random.fold_in(key, axis), (), 0, length) for axis, length in enumerate(entries.shape)]
    widest = entries.shape.index(max(entries.shape))
    beside = place[:widest] + [(place[widest] + 1) % entries.shape[widest]] + place[widest + 1:]
    return entries.at[tuple(place)].set(least).at[tuple(beside)].set(largest)


def steps_of(rng, shape, shards, least, largest):
    gain, own = 1.0, jax.random.fold_in(rng, 6)
    for axis_at, shards_of in shards:
        draws = jnp.exp(jax.random.uniform(jax.random.fold_in(own, axis_at), (shards_of,), jnp.float32, least / len(shards), largest / len(shards)))
        gain = gain * jnp.repeat(draws, shape[axis_at] // shards_of).reshape([-1 if axis == axis_at else 1 for axis in range(len(shape))])
    return gain


def rank_bounds(number_of, skew):
    portions = [(1 << 20) // math.isqrt(grade ** skew) + 1 for grade in range(1, number_of + 1)]
    scale = 1 + sum(portions) // (1 << 30)
    return np.cumsum(np.array([max(1, weight // scale) for weight in portions]))


def ranked(own_key, extent, amount, lean):
    listing = rank_bounds(amount, lean)
    pick = jax.random.randint(jax.random.fold_in(own_key, 1), extent, 0, int(listing[amount - 1]))
    rank = jnp.searchsorted(jnp.asarray(listing, jnp.int32), pick, side="right")
    return jax.random.permutation(jax.random.fold_in(own_key, 2), amount)[rank].astype(jnp.int32)


def scatter_about(rng, dims, scale, reach, cuts=(), kind=jnp.bfloat16):
    values = scale * jax.random.normal(rng, dims, jnp.float32)
    if cuts:
        values = values * steps_of(rng, dims, cuts, -0.22, 0.18)
    return jnp.clip(values, -reach, reach).astype(kind)


def setup_inputs(seed: int = 0) -> dict:
    key_of = jax.random.split(jax.random.key(seed), 9)
    return {
        "cold_table": scatter_about(key_of[0], (VROWS, E), 1.0, 6.0, ((0, 4),)),
        "slot_row": draw_slot_row(jax.random.fold_in(key_of[8], 71), 0),
        "slot_sample": draw_slot_sample(jax.random.fold_in(key_of[8], 71), 0),
        "slot_count": draw_slot_count(jax.random.fold_in(key_of[8], 71), 0),
        "hot_table": scatter_about(key_of[4], (HOT, E), 1.0, 6.0),
        "hot_index": place_ends(ranked(key_of[5], (SAMPLES, KH), HOT, 1), jax.random.fold_in(key_of[5], 3), 0, HOT - 1).astype(jnp.int32),
        "hot_count": place_ends(jax.random.randint(key_of[6], (SAMPLES, KH), 1, 16), jax.random.fold_in(key_of[6], 1), 1, 15).astype(jnp.int32),
        "hot_cotangent": scatter_about(key_of[7], (SAMPLES, E), 0.1, 0.59765625, ((0, 32),)),
    }


cold_scale = 0.03125
hot_scale = 0.0625

def reference(cold_table, slot_row, slot_sample, slot_count, hot_table, hot_index, hot_count, hot_cotangent):
    sources = slot_row.shape[0] // PEERS
    owner_base = (jnp.arange(PEERS, dtype=jnp.int32) * V_SHARD)[:, None]

    def pool_cold(packed):
        local_rows, sample_idx, counts = packed
        picked = jnp.take(cold_table, (local_rows + owner_base).reshape(-1), axis=0).astype(jnp.float32)
        weights = counts.reshape(-1).astype(jnp.float32) * cold_scale
        return jax.ops.segment_sum(picked * weights[:, None], sample_idx.reshape(-1), num_segments=S_DEV)
    cold_pooled = lax.map(pool_cold, (slot_row.reshape(sources, PEERS, CAP), slot_sample.reshape(sources, PEERS, CAP), slot_count.reshape(sources, PEERS, CAP)))
    cold_pooled = cold_pooled.reshape(SAMPLES, E).astype(jnp.bfloat16)
    index_blocks = hot_index.reshape(sources, S_DEV, KH)
    count_blocks = hot_count.reshape(sources, S_DEV, KH)
    grad_blocks = hot_cotangent.reshape(sources, S_DEV, E)

    def pool_hot(packed):
        indices, counts = packed
        picked = jnp.take(hot_table, indices.reshape(-1), axis=0).astype(jnp.float32).reshape(S_DEV, KH, E)
        return lax.optimization_barrier(jnp.sum(picked * (counts.astype(jnp.float32) * hot_scale)[:, :, None], axis=1))
    hot_pooled = lax.map(pool_hot, (index_blocks, count_blocks)).reshape(SAMPLES, E).astype(jnp.bfloat16)

    def add_grad(total, packed):
        indices, counts, grads = packed
        weighted = grads.astype(jnp.float32)[:, None, :] * (counts.astype(jnp.float32) * hot_scale)[:, :, None]
        return (total + jax.ops.segment_sum(weighted.reshape(-1, E), indices.reshape(-1), num_segments=HOT), None)
    hot_grad, _ = lax.scan(add_grad, jnp.zeros((HOT, E), jnp.float32), (index_blocks, count_blocks, grad_blocks))
    features = jnp.concatenate([cold_pooled, hot_pooled], axis=1)
    return (features, hot_grad)
```

```python
import functools

import jax
import jax.numpy as jnp
from jax import lax
from jax.experimental import pallas as pl
from jax.experimental.pallas import tpu as pltpu
from jax.sharding import PartitionSpec as P

MESH = pl.DeviceIdType.MESH
cold_scale = 0.03125
hot_scale = 0.0625
LANES = 128
TABLE_CHUNKS = 8
GROUP = 32


def kernel(
    tables,
    blks,
    table_hbm,
    req_ref,
    hot_ref,
    index_ref,
    count_ref,
    cot_ref,
    feat_ref,
    grad_ref,
    staged,
    wide,
    req_in,
    rows_smem,
    inc,
    grad_all,
    core_in,
    halves,
    table_in,
    quarter,
    z_in,
    gathered,
    weights,
    pooled,
    pooled_in,
    total,
    shares,
    stage_sem,
    smem_sem,
    req_send,
    req_recv,
    core_sem,
    tab_send,
    tab_recv,
    z_send,
    z_recv,
    ag_send,
    ag_recv,
    pool_send,
    pool_recv,
):
    me_t = lax.axis_index("table")
    me_b = lax.axis_index("blk")
    core = lax.rem(me_b, 2)
    me_z = me_b // 2
    zs = blks // 2
    samples = cot_ref.shape[0]
    hot_rows = hot_ref.shape[0]
    block = hot_rows // blks
    share = block // tables
    req_rows = req_ref.shape[2]
    chunk = table_hbm.shape[0] // TABLE_CHUNKS

    stage_copies = []
    for i in range(TABLE_CHUNKS):
        part = pl.ds(i * chunk, chunk)
        copy = pltpu.make_async_copy(table_hbm.at[part], staged.at[part], stage_sem.at[i])
        copy.start()
        stage_copies.append(copy)

    def table_peer(k):
        return (lax.rem(me_t + k, tables), me_b)

    def z_peer(k):
        return (me_t, lax.rem(me_z + k, zs) * 2 + core)

    core_peer = (me_t, me_z * 2 + 1 - core)
    partners = [table_peer(k) for k in range(1, tables)]
    partners += [z_peer(k) for k in range(1, zs)] + [core_peer]
    barrier = pltpu.get_barrier_semaphore()
    for partner in partners:
        pl.semaphore_signal(barrier, inc=1, device_id=partner, device_id_type=MESH)
    pl.semaphore_wait(barrier, len(partners))

    def send(src, dst, send_sem, recv_sem, to):
        copy = pltpu.make_async_remote_copy(
            src_ref=src,
            dst_ref=dst,
            send_sem=send_sem,
            recv_sem=recv_sem,
            device_id=to,
            device_id_type=MESH,
        )
        copy.start()
        return copy

    req_copies = [
        send(
            req_ref.at[lax.rem(me_t + k, tables)],
            req_in.at[k - 1],
            req_send.at[k - 1],
            req_recv.at[k - 1],
            table_peer(k),
        )
        for k in range(1, tables)
    ]

    tile = 64
    for lane in range(samples // LANES):
        cols = pl.ds(lane * LANES, LANES)
        lookups = index_ref.shape[0]
        idx = [index_ref[k : k + 1, cols] for k in range(lookups)]
        wts = [count_ref[k : k + 1, cols].astype(jnp.float32) * hot_scale for k in range(lookups)]
        ids = lax.broadcasted_iota(jnp.int32, (tile, LANES), 0)

        def add_tile(r, carry):
            base = pl.multiple_of(r * tile, tile)
            here = ids + base
            acc = jnp.where(here == idx[0], wts[0], 0.0)
            for k in range(1, lookups):
                acc = acc + jnp.where(here == idx[k], wts[k], 0.0)
            inc[pl.ds(base, tile), cols] = acc.astype(jnp.bfloat16)
            return carry

        lax.fori_loop(0, hot_rows // tile, add_tile, 0)

    def grad_block(b, carry):
        base = pl.multiple_of(b * block, block)
        grad_all[lax.rem(b, 2), b // 2] = jnp.dot(
            inc[pl.ds(base, block), :], cot_ref[...], preferred_element_type=jnp.float32
        )
        return carry

    lax.fori_loop(0, blks, grad_block, 0)
    core_copy = send(grad_all.at[1 - core], core_in, core_sem.at[0], core_sem.at[1], core_peer)

    hot_t = lax.dot_general(
        hot_ref[...], inc[...], (((0,), (0,)), ((), ())), preferred_element_type=jnp.float32
    )
    width = hot_ref.shape[1]
    feat_ref[:, width:] = hot_t.T.astype(jnp.bfloat16)

    own_copy = pltpu.make_async_copy(req_ref.at[me_t, 0], rows_smem.at[tables - 1], smem_sem.at[tables - 1])
    own_copy.start()
    smem_copies = []
    for k in range(1, tables):
        req_copies[k - 1].wait()
        copy = pltpu.make_async_copy(req_in.at[k - 1, 0], rows_smem.at[k - 1], smem_sem.at[k - 1])
        copy.start()
        smem_copies.append(copy)
    smem_copies.append(own_copy)

    step = 256
    for i in range(TABLE_CHUNKS):
        stage_copies[i].wait()

        def widen(r, carry):
            part = pl.ds(pl.multiple_of(i * chunk + r * step, step), step)
            wide[part, :] = staged[part, :].astype(jnp.float32)
            return carry

        lax.fori_loop(0, chunk // step, widen, 0)
    for copy in smem_copies:
        copy.wait()

    def pool(slot, load_meta):
        def body(i, carry):
            base = pl.multiple_of(i * LANES, LANES)
            sample = load_meta(1, i)
            weight = load_meta(2, i).astype(jnp.float32) * cold_scale
            for s in range(samples // LANES):
                ids = lax.broadcasted_iota(jnp.int32, (LANES, LANES), 0) + s * LANES
                weights[pl.ds(s * LANES, LANES), pl.ds(base, LANES)] = jnp.where(
                    ids == sample, weight, 0.0
                ).astype(jnp.bfloat16)
            for g in range(0, LANES, GROUP):
                got = [wide[pl.ds(rows_smem[slot, i, g + j], 1), :] for j in range(GROUP)]
                for j in range(GROUP):
                    gathered[pl.ds(base + g + j, 1), :] = got[j]
            return carry

        lax.fori_loop(0, req_rows, body, 0)
        return jnp.dot(
            weights[...], gathered[...].astype(jnp.bfloat16), preferred_element_type=jnp.float32
        )

    def pool_peer(k):
        pooled[k - 1] = pool(k - 1, lambda f, i: req_in[k - 1, f, pl.ds(i, 1), :])
        return send(
            pooled.at[k - 1],
            pooled_in.at[k - 1],
            pool_send.at[k - 1],
            pool_recv.at[k - 1],
            (lax.rem(me_t + tables - k, tables), me_b),
        )

    def core_stage():
        core_copy.wait()
        for part in range(tables):
            rows = pl.ds(part * share, share)
            halves[part] = grad_all[core, :, rows, :] + core_in[:, rows, :]
        return [
            send(
                halves.at[lax.rem(me_t + k, tables)],
                table_in.at[k - 1],
                tab_send.at[k - 1],
                tab_recv.at[k - 1],
                table_peer(k),
            )
            for k in range(1, tables)
        ]

    def table_stage(copies):
        for copy in copies:
            copy.wait()
        acc = halves[me_t]
        for k in range(1, tables):
            acc = acc + table_in[k - 1]
        quarter[...] = acc
        return [
            send(
                quarter.at[lax.rem(me_z + k, zs)],
                z_in.at[k - 1],
                z_send.at[k - 1],
                z_recv.at[k - 1],
                z_peer(k),
            )
            for k in range(1, zs)
        ]

    def z_stage(copies):
        for copy in copies:
            copy.wait()
        acc = quarter[me_z]
        for k in range(1, zs):
            acc = acc + z_in[k - 1]
        total[...] = acc
        return [
            send(total, shares.at[k - 1], ag_send.at[k - 1], ag_recv.at[k - 1], table_peer(k))
            for k in range(1, tables)
        ]

    def gather_stage(copies):
        for copy in copies:
            copy.wait()
        grad_ref[pl.ds(pl.multiple_of(me_t * share, share), share), :] = total[...]
        for k in range(1, tables):
            source = lax.rem(me_t + tables - k, tables)
            grad_ref[pl.ds(pl.multiple_of(source * share, share), share), :] = shares[k - 1]

    pool_copies = []
    state = core_stage()
    stages = [table_stage, z_stage, gather_stage]
    for k in range(1, tables):
        pool_copies.append(pool_peer(k))
        if k - 1 < len(stages):
            state = stages[k - 1](state)
    cold = pool(tables - 1, lambda f, i: req_ref[me_t, f, pl.ds(i, 1), :])
    for copy in pool_copies:
        copy.wait()
    for k in range(1, tables):
        cold = cold + pooled_in[k - 1]
    feat_ref[:, :width] = cold.astype(jnp.bfloat16)


def shards(
    tables,
    blks,
    cold_table,
    slot_row,
    slot_sample,
    slot_count,
    hot_table,
    hot_index,
    hot_count,
    hot_cotangent,
):
    slots = slot_row.shape[1]
    req_rows = slots // LANES
    requests = jnp.stack([slot_row, slot_sample, slot_count], axis=1).reshape(
        tables, 3, req_rows, LANES
    )
    samples, width = hot_cotangent.shape
    hot_rows = hot_table.shape[0]
    zs = blks // 2
    block = hot_rows // blks
    share = block // tables
    f32 = jnp.float32
    dma = pltpu.SemaphoreType.DMA
    vmem = pl.BlockSpec(memory_space=pltpu.VMEM)
    return pl.pallas_call(
        functools.partial(kernel, tables, blks),
        out_shape=(
            jax.ShapeDtypeStruct((samples, 2 * width), jnp.bfloat16),
            jax.ShapeDtypeStruct((block, width), f32),
        ),
        in_specs=[pl.BlockSpec(memory_space=pl.ANY)] + [vmem] * 5,
        out_specs=(vmem, vmem),
        scratch_shapes=[
            pltpu.VMEM(cold_table.shape, jnp.bfloat16),
            pltpu.VMEM(cold_table.shape, f32),
            pltpu.VMEM((tables - 1, 3, req_rows, LANES), jnp.int32),
            pltpu.SMEM((tables, req_rows, LANES), jnp.int32),
            pltpu.VMEM((hot_rows, samples), jnp.bfloat16),
            pltpu.VMEM((2, zs, block, width), f32),
            pltpu.VMEM((zs, block, width), f32),
            pltpu.VMEM((tables, zs, share, width), f32),
            pltpu.VMEM((tables - 1, zs, share, width), f32),
            pltpu.VMEM((zs, share, width), f32),
            pltpu.VMEM((zs - 1, share, width), f32),
            pltpu.VMEM((slots, width), f32),
            pltpu.VMEM((samples, slots), jnp.bfloat16),
            pltpu.VMEM((tables - 1, samples, width), f32),
            pltpu.VMEM((tables - 1, samples, width), f32),
            pltpu.VMEM((share, width), f32),
            pltpu.VMEM((tables - 1, share, width), f32),
            dma((TABLE_CHUNKS,)),
            dma((tables,)),
            dma((tables - 1,)),
            dma((tables - 1,)),
            dma((2,)),
            dma((tables - 1,)),
            dma((tables - 1,)),
            dma((zs - 1,)),
            dma((zs - 1,)),
            dma((tables - 1,)),
            dma((tables - 1,)),
            dma((tables - 1,)),
            dma((tables - 1,)),
        ],
        compiler_params=pltpu.CompilerParams(
            collective_id=0, has_side_effects=True, vmem_limit_bytes=56 * 1024 * 1024
        ),
    )(cold_table, requests, hot_table, hot_index.T, hot_count.T, hot_cotangent)


def solution(mesh):
    both = P(("table", "blk"), None)
    return jax.shard_map(
        functools.partial(shards, mesh.shape["table"], mesh.shape["blk"]),
        mesh=mesh,
        in_specs=(P("table", None), both, both, both, P(), both, both, both),
        out_specs=(both, P("blk", None)),
        check_vma=False,
    )
```

```python
import functools

import jax
import jax.numpy as jnp
from jax import lax
from jax.experimental import pallas as pl
from jax.experimental.pallas import tpu as pltpu
from jax.sharding import PartitionSpec as P

MESH = pl.DeviceIdType.MESH
cold_scale = 0.03125
hot_scale = 0.0625
LANES = 128
GROUP = 32


def kernel(
    tables,
    blks,
    table_hbm,
    row_ref,
    sample_ref,
    slot_count_ref,
    hot_ref,
    index_ref,
    count_ref,
    cot_ref,
    feat_ref,
    grad_ref,
    staged,
    wide,
    req_ref,
    req_in,
    rows_smem,
    inc,
    grad_all,
    core_in,
    halves,
    table_in,
    quarter,
    z_in,
    gathered,
    weights,
    pooled,
    pooled_in,
    total,
    shares,
    stage_sem,
    smem_sem,
    req_send,
    req_recv,
    core_sem,
    tab_send,
    tab_recv,
    z_send,
    z_recv,
    ag_send,
    ag_recv,
    pool_send,
    pool_recv,
):
    me_t = lax.axis_index("table")
    me_b = lax.axis_index("blk")
    core = lax.rem(me_b, 2)
    me_z = me_b // 2
    zs = blks // 2
    samples = cot_ref.shape[0]
    hot_rows = hot_ref.shape[0]
    block = hot_rows // blks
    share = block // tables
    req_rows = req_ref.shape[2]
    chunks = stage_sem.shape[0]
    chunk = table_hbm.shape[0] // chunks

    stage_copies = []
    for i in range(chunks):
        part = pl.ds(i * chunk, chunk)
        copy = pltpu.make_async_copy(table_hbm.at[part], staged.at[part], stage_sem.at[i])
        copy.start()
        stage_copies.append(copy)

    def table_peer(k):
        return (me_t ^ k, me_b)

    def z_peer(k):
        return (me_t, lax.rem(me_z + k, zs) * 2 + core)

    core_peer = (me_t, me_z * 2 + 1 - core)
    partners = [table_peer(k) for k in range(1, tables)]
    partners += [z_peer(k) for k in range(1, zs)] + [core_peer]
    barrier = pltpu.get_barrier_semaphore()
    for partner in partners:
        pl.semaphore_signal(barrier, inc=1, device_id=partner, device_id_type=MESH)
    for f, ref in enumerate((row_ref, sample_ref, slot_count_ref)):
        for peer in range(tables):
            for i in range(req_rows):
                req_ref[peer, f, i : i + 1, :] = ref[peer : peer + 1, i * LANES : (i + 1) * LANES]
    pl.semaphore_wait(barrier, len(partners))

    def send(src, dst, send_sem, recv_sem, to):
        copy = pltpu.make_async_remote_copy(
            src_ref=src,
            dst_ref=dst,
            send_sem=send_sem,
            recv_sem=recv_sem,
            device_id=to,
            device_id_type=MESH,
        )
        copy.start()
        return copy

    req_copies = [
        send(
            req_ref.at[me_t ^ k],
            req_in.at[k - 1],
            req_send.at[k - 1],
            req_recv.at[k - 1],
            table_peer(k),
        )
        for k in range(1, tables)
    ]

    tile = 64
    for lane in range(samples // LANES):
        cols = pl.ds(lane * LANES, LANES)
        lookups = index_ref.shape[0]
        idx = [index_ref[k : k + 1, cols] for k in range(lookups)]
        wts = [count_ref[k : k + 1, cols].astype(jnp.float32) * hot_scale for k in range(lookups)]
        ids = lax.broadcasted_iota(jnp.int32, (tile, LANES), 0)

        per_chunk = hot_rows // tile // 2
        wide_rows = chunk // per_chunk
        for half in range(2):
            c = lane * 2 + half
            stage_copies[c].wait()

            def add_tile(r, carry):
                base = pl.multiple_of((half * per_chunk + r) * tile, tile)
                part = pl.ds(pl.multiple_of(c * chunk + r * wide_rows, wide_rows), wide_rows)
                wide[part, :] = staged[part, :].astype(jnp.float32)
                here = ids + base
                acc = jnp.where(here == idx[0], wts[0], 0.0)
                for k in range(1, lookups):
                    acc = acc + jnp.where(here == idx[k], wts[k], 0.0)
                inc[pl.ds(base, tile), cols] = acc.astype(jnp.bfloat16)
                return carry

            lax.fori_loop(0, per_chunk, add_tile, 0)

    def grad_block(b, carry):
        base = pl.multiple_of(b * block, block)
        grad_all[lax.rem(b, 2), b // 2] = jnp.dot(
            inc[pl.ds(base, block), :], cot_ref[...], preferred_element_type=jnp.float32
        )
        return carry

    lax.fori_loop(0, blks, grad_block, 0)
    core_copy = send(grad_all.at[1 - core], core_in, core_sem.at[0], core_sem.at[1], core_peer)

    hot_t = lax.dot_general(
        hot_ref[...], inc[...], (((0,), (0,)), ((), ())), preferred_element_type=jnp.float32
    )
    width = hot_ref.shape[1]
    feat_ref[:, width:] = hot_t.T.astype(jnp.bfloat16)

    own_copy = pltpu.make_async_copy(req_ref.at[me_t, 0], rows_smem.at[tables - 1], smem_sem.at[tables - 1])
    own_copy.start()
    smem_copies = []
    for k in range(1, tables):
        req_copies[k - 1].wait()
        copy = pltpu.make_async_copy(req_in.at[k - 1, 0], rows_smem.at[k - 1], smem_sem.at[k - 1])
        copy.start()
        smem_copies.append(copy)
    smem_copies.append(own_copy)

    for copy in smem_copies:
        copy.wait()

    def pool(slot, load_meta):
        def body(i, carry):
            base = pl.multiple_of(i * LANES, LANES)
            sample = load_meta(1, i)
            weight = load_meta(2, i).astype(jnp.float32) * cold_scale
            for s in range(samples // LANES):
                ids = lax.broadcasted_iota(jnp.int32, (LANES, LANES), 0) + s * LANES
                weights[pl.ds(s * LANES, LANES), pl.ds(base, LANES)] = jnp.where(
                    ids == sample, weight, 0.0
                ).astype(jnp.bfloat16)
            for g in range(0, LANES, GROUP):
                got = [wide[pl.ds(rows_smem[slot, i, g + j], 1), :] for j in range(GROUP)]
                for j in range(GROUP):
                    gathered[i, g + j : g + j + 1, :] = got[j]
            return carry

        lax.fori_loop(0, req_rows, body, 0)
        picked = gathered[...].reshape(req_rows * LANES, width).astype(jnp.bfloat16)
        return jnp.dot(weights[...], picked, preferred_element_type=jnp.float32)

    def pool_peer(k):
        pooled[k - 1] = pool(k - 1, lambda f, i: req_in[k - 1, f, pl.ds(i, 1), :])
        return send(
            pooled.at[k - 1],
            pooled_in.at[k - 1],
            pool_send.at[k - 1],
            pool_recv.at[k - 1],
            table_peer(k),
        )

    def core_stage():
        core_copy.wait()
        for part in range(tables):
            rows = pl.ds(part * share, share)
            halves[part] = grad_all[core, :, rows, :] + core_in[:, rows, :]
        return [
            send(
                halves.at[me_t ^ k],
                table_in.at[k - 1],
                tab_send.at[k - 1],
                tab_recv.at[k - 1],
                table_peer(k),
            )
            for k in range(1, tables)
        ]

    def table_stage(copies):
        for copy in copies:
            copy.wait()
        acc = halves[me_t]
        for k in range(1, tables):
            acc = acc + table_in[k - 1]
        quarter[...] = acc
        return [
            send(
                quarter.at[lax.rem(me_z + k, zs)],
                z_in.at[k - 1],
                z_send.at[k - 1],
                z_recv.at[k - 1],
                z_peer(k),
            )
            for k in range(1, zs)
        ]

    def z_stage(copies):
        for copy in copies:
            copy.wait()
        acc = quarter[me_z]
        for k in range(1, zs):
            acc = acc + z_in[k - 1]
        total[...] = acc
        return [
            send(total, shares.at[k - 1], ag_send.at[k - 1], ag_recv.at[k - 1], table_peer(k))
            for k in range(1, tables)
        ]

    def gather_stage(copies):
        for copy in copies:
            copy.wait()
        grad_ref[pl.ds(pl.multiple_of(me_t * share, share), share), :] = total[...]
        for k in range(1, tables):
            source = me_t ^ k
            grad_ref[pl.ds(pl.multiple_of(source * share, share), share), :] = shares[k - 1]

    pool_copies = []
    state = core_stage()
    stages = [table_stage, z_stage, gather_stage]
    for n, k in enumerate(reversed(range(1, tables))):
        pool_copies.append(pool_peer(k))
        if n < len(stages):
            state = stages[n](state)
    cold = pool(tables - 1, lambda f, i: req_ref[me_t, f, pl.ds(i, 1), :])
    for copy in pool_copies:
        copy.wait()
    for k in range(1, tables):
        cold = cold + pooled_in[k - 1]
    feat_ref[:, :width] = cold.astype(jnp.bfloat16)


def hand_out(feat_ref, grad_ref, feat_out, grad_out, sems):
    copies = [
        pltpu.make_async_copy(feat_ref, feat_out, sems.at[0]),
        pltpu.make_async_copy(grad_ref, grad_out, sems.at[1]),
    ]
    for copy in copies:
        copy.start()
    for copy in copies:
        copy.wait()


def shards(
    tables,
    blks,
    cold_table,
    slot_row,
    slot_sample,
    slot_count,
    hot_table,
    hot_index,
    hot_count,
    hot_cotangent,
):
    slots = slot_row.shape[1]
    req_rows = slots // LANES
    samples, width = hot_cotangent.shape
    hot_rows = hot_table.shape[0]
    zs = blks // 2
    block = hot_rows // blks
    share = block // tables
    f32 = jnp.float32
    dma = pltpu.SemaphoreType.DMA
    vmem = pl.BlockSpec(memory_space=pltpu.VMEM)
    features, hot_grad = pl.pallas_call(
        functools.partial(kernel, tables, blks),
        out_shape=(
            jax.ShapeDtypeStruct((samples, 2 * width), jnp.bfloat16),
            jax.ShapeDtypeStruct((block, width), f32),
        ),
        in_specs=[pl.BlockSpec(memory_space=pl.ANY)] + [vmem] * 7,
        out_specs=(vmem, vmem),
        scratch_shapes=[
            pltpu.VMEM(cold_table.shape, jnp.bfloat16),
            pltpu.VMEM(cold_table.shape, f32),
            pltpu.VMEM((tables, 3, req_rows, LANES), jnp.int32),
            pltpu.VMEM((tables - 1, 3, req_rows, LANES), jnp.int32),
            pltpu.SMEM((tables, req_rows, LANES), jnp.int32),
            pltpu.VMEM((hot_rows, samples), jnp.bfloat16),
            pltpu.VMEM((2, zs, block, width), f32),
            pltpu.VMEM((zs, block, width), f32),
            pltpu.VMEM((tables, zs, share, width), f32),
            pltpu.VMEM((tables - 1, zs, share, width), f32),
            pltpu.VMEM((zs, share, width), f32),
            pltpu.VMEM((zs - 1, share, width), f32),
            pltpu.VMEM((req_rows, LANES, width), f32),
            pltpu.VMEM((samples, slots), jnp.bfloat16),
            pltpu.VMEM((tables - 1, samples, width), f32),
            pltpu.VMEM((tables - 1, samples, width), f32),
            pltpu.VMEM((share, width), f32),
            pltpu.VMEM((tables - 1, share, width), f32),
            dma((2 * (samples // LANES),)),
            dma((tables,)),
            dma((tables - 1,)),
            dma((tables - 1,)),
            dma((2,)),
            dma((tables - 1,)),
            dma((tables - 1,)),
            dma((zs - 1,)),
            dma((zs - 1,)),
            dma((tables - 1,)),
            dma((tables - 1,)),
            dma((tables - 1,)),
            dma((tables - 1,)),
        ],
        compiler_params=pltpu.CompilerParams(
            collective_id=0, has_side_effects=True, vmem_limit_bytes=56 * 1024 * 1024
        ),
    )(
        cold_table,
        slot_row,
        slot_sample,
        slot_count,
        hot_table,
        hot_index.T,
        hot_count.T,
        hot_cotangent,
    )
    features, hot_grad = pl.pallas_call(
        hand_out,
        out_shape=(
            jax.ShapeDtypeStruct(features.shape, features.dtype),
            jax.ShapeDtypeStruct(hot_grad.shape, hot_grad.dtype),
        ),
        in_specs=[pl.BlockSpec(memory_space=pl.ANY)] * 2,
        out_specs=[pl.BlockSpec(memory_space=pl.ANY)] * 2,
        scratch_shapes=[dma((2,))],
    )(features, hot_grad)
    return features, hot_grad


def solution(mesh):
    both = P(("table", "blk"), None)
    return jax.shard_map(
        functools.partial(shards, mesh.shape["table"], mesh.shape["blk"]),
        mesh=mesh,
        in_specs=(P("table", None), both, both, both, P(), both, both, both),
        out_specs=(both, P("blk", None)),
        check_vma=False,
    )
```

```python
import functools

import jax
import jax.numpy as jnp
from jax import lax
from jax.experimental import pallas as pl
from jax.experimental.pallas import tpu as pltpu
from jax.sharding import PartitionSpec as P

MESH = pl.DeviceIdType.MESH
cold_scale = 0.03125
hot_scale = 0.0625
LANES = 128
AHEAD = 24
PIECE = 16


def kernel(
    tables,
    blks,
    table_hbm,
    row_ref,
    sample_ref,
    slot_count_ref,
    hot_ref,
    index_ref,
    count_ref,
    cot_ref,
    feat_ref,
    grad_ref,
    staged,
    wide,
    req_ref,
    req_in,
    rows_smem,
    inc,
    grad_all,
    core_in,
    halves,
    table_in,
    quarter,
    z_in,
    gathered,
    weights,
    pooled,
    pooled_in,
    total,
    shares,
    stage_sem,
    smem_sem,
    req_send,
    req_recv,
    core_sem,
    tab_send,
    tab_recv,
    z_send,
    z_recv,
    ag_send,
    ag_recv,
    pool_send,
    pool_recv,
):
    me_t = lax.axis_index("table")
    me_b = lax.axis_index("blk")
    core = lax.rem(me_b, 2)
    me_z = me_b // 2
    zs = blks // 2
    samples = cot_ref.shape[0]
    hot_rows = hot_ref.shape[0]
    block = hot_rows // blks
    share = block // tables
    req_rows = req_ref.shape[2]
    chunks = stage_sem.shape[0]
    chunk = table_hbm.shape[0] // chunks

    stage_copies = []
    for i in range(chunks):
        part = pl.ds(i * chunk, chunk)
        copy = pltpu.make_async_copy(table_hbm.at[part], staged.at[part], stage_sem.at[i])
        copy.start()
        stage_copies.append(copy)

    def table_peer(k):
        return (me_t ^ k, me_b)

    def z_peer(k):
        return (me_t, lax.rem(me_z + k, zs) * 2 + core)

    core_peer = (me_t, me_z * 2 + 1 - core)
    partners = [table_peer(k) for k in range(1, tables)]
    partners += [z_peer(k) for k in range(1, zs)] + [core_peer]
    barrier = pltpu.get_barrier_semaphore()
    for partner in partners:
        pl.semaphore_signal(barrier, inc=1, device_id=partner, device_id_type=MESH)
    for f, ref in enumerate((row_ref, sample_ref, slot_count_ref)):
        for peer in range(tables):
            for i in range(req_rows):
                req_ref[peer, f, i : i + 1, :] = ref[peer : peer + 1, i * LANES : (i + 1) * LANES]
    pl.semaphore_wait(barrier, len(partners))

    def send(src, dst, send_sem, recv_sem, to):
        copy = pltpu.make_async_remote_copy(
            src_ref=src,
            dst_ref=dst,
            send_sem=send_sem,
            recv_sem=recv_sem,
            device_id=to,
            device_id_type=MESH,
        )
        copy.start()
        return copy

    req_copies = [
        send(
            req_ref.at[me_t ^ k],
            req_in.at[k - 1],
            req_send.at[k - 1],
            req_recv.at[k - 1],
            table_peer(k),
        )
        for k in range(1, tables)
    ]

    tile = 64
    for lane in range(samples // LANES):
        cols = pl.ds(lane * LANES, LANES)
        lookups = index_ref.shape[0]
        idx = [index_ref[k : k + 1, cols] for k in range(lookups)]
        wts = [count_ref[k : k + 1, cols].astype(jnp.float32) * hot_scale for k in range(lookups)]
        ids = lax.broadcasted_iota(jnp.int32, (tile, LANES), 0)

        per_chunk = hot_rows // tile // 2
        wide_rows = chunk // per_chunk
        for half in range(2):
            c = lane * 2 + half
            stage_copies[c].wait()

            def add_tile(r, carry):
                base = pl.multiple_of((half * per_chunk + r) * tile, tile)
                part = pl.ds(pl.multiple_of(c * chunk + r * wide_rows, wide_rows), wide_rows)
                wide[part, :] = staged[part, :].astype(jnp.float32)
                here = ids + base
                acc = jnp.where(here == idx[0], wts[0], 0.0)
                for k in range(1, lookups):
                    acc = acc + jnp.where(here == idx[k], wts[k], 0.0)
                inc[pl.ds(base, tile), cols] = acc.astype(jnp.bfloat16)
                return carry

            lax.fori_loop(0, per_chunk, add_tile, 0)

    def grad_block(b, carry):
        base = pl.multiple_of(b * block, block)
        grad_all[lax.rem(b, 2), b // 2] = jnp.dot(
            inc[pl.ds(base, block), :], cot_ref[...], preferred_element_type=jnp.float32
        )
        return carry

    lax.fori_loop(0, blks, grad_block, 0)
    core_copy = send(grad_all.at[1 - core], core_in, core_sem.at[0], core_sem.at[1], core_peer)

    hot_t = lax.dot_general(
        hot_ref[...], inc[...], (((0,), (0,)), ((), ())), preferred_element_type=jnp.float32
    )
    width = hot_ref.shape[1]
    feat_ref[:, width:] = hot_t.T.astype(jnp.bfloat16)

    own_copy = pltpu.make_async_copy(req_ref.at[me_t, 0], rows_smem.at[tables - 1], smem_sem.at[tables - 1])
    own_copy.start()
    smem_copies = []
    for k in range(1, tables):
        req_copies[k - 1].wait()
        copy = pltpu.make_async_copy(req_in.at[k - 1, 0], rows_smem.at[k - 1], smem_sem.at[k - 1])
        copy.start()
        smem_copies.append(copy)
    smem_copies.append(own_copy)

    for copy in smem_copies:
        copy.wait()

    def pool(slot, load_meta):
        def body(i, carry):
            base = pl.multiple_of(i * LANES, LANES)
            sample = load_meta(1, i)
            weight = load_meta(2, i).astype(jnp.float32) * cold_scale
            sample = jnp.broadcast_to(sample, (8, LANES))
            weight = jnp.broadcast_to(weight, (8, LANES))
            ids = lax.broadcasted_iota(jnp.int32, (8, LANES), 0)
            pieces = samples // PIECE
            got, done = [], 0
            for j in range(LANES + AHEAD):
                if j < LANES:
                    got.append(wide[pl.ds(rows_smem[slot, i, j], 1), :])
                if j >= AHEAD:
                    at = j - AHEAD
                    gathered[i, at : at + 1, :] = got[at]
                while j < LANES and done < (j + 1) * pieces // LANES:
                    first = done * PIECE
                    piece = [
                        jnp.where(ids + (first + r) == sample, weight, 0.0)
                        for r in range(0, PIECE, 8)
                    ]
                    weights[first : first + PIECE, pl.ds(base, LANES)] = jnp.concatenate(
                        piece, axis=0
                    ).astype(jnp.bfloat16)
                    done += 1
            return carry

        lax.fori_loop(0, req_rows, body, 0)
        picked = gathered[...].reshape(req_rows * LANES, width).astype(jnp.bfloat16)
        return jnp.dot(weights[...], picked, preferred_element_type=jnp.float32)

    def pool_peer(k):
        pooled[k - 1] = pool(k - 1, lambda f, i: req_in[k - 1, f, pl.ds(i, 1), :])
        return send(
            pooled.at[k - 1],
            pooled_in.at[k - 1],
            pool_send.at[k - 1],
            pool_recv.at[k - 1],
            table_peer(k),
        )

    def core_stage():
        core_copy.wait()
        for part in range(tables):
            rows = pl.ds(part * share, share)
            halves[part] = grad_all[core, :, rows, :] + core_in[:, rows, :]
        return [
            send(
                halves.at[me_t ^ k],
                table_in.at[k - 1],
                tab_send.at[k - 1],
                tab_recv.at[k - 1],
                table_peer(k),
            )
            for k in range(1, tables)
        ]

    def table_stage(copies):
        for copy in copies:
            copy.wait()
        acc = halves[me_t]
        for k in range(1, tables):
            acc = acc + table_in[k - 1]
        quarter[...] = acc
        return [
            send(
                quarter.at[lax.rem(me_z + k, zs)],
                z_in.at[k - 1],
                z_send.at[k - 1],
                z_recv.at[k - 1],
                z_peer(k),
            )
            for k in range(1, zs)
        ]

    def z_stage(copies):
        for copy in copies:
            copy.wait()
        acc = quarter[me_z]
        for k in range(1, zs):
            acc = acc + z_in[k - 1]
        total[...] = acc
        return [
            send(total, shares.at[k - 1], ag_send.at[k - 1], ag_recv.at[k - 1], table_peer(k))
            for k in range(1, tables)
        ]

    def gather_stage(copies):
        for copy in copies:
            copy.wait()
        grad_ref[pl.ds(pl.multiple_of(me_t * share, share), share), :] = total[...]
        for k in range(1, tables):
            source = me_t ^ k
            grad_ref[pl.ds(pl.multiple_of(source * share, share), share), :] = shares[k - 1]

    pool_copies = []
    state = core_stage()
    stages = [table_stage, z_stage, gather_stage]
    for n, k in enumerate(reversed(range(1, tables))):
        pool_copies.append(pool_peer(k))
        if n < len(stages):
            state = stages[n](state)
    cold = pool(tables - 1, lambda f, i: req_ref[me_t, f, pl.ds(i, 1), :])
    for copy in pool_copies:
        copy.wait()
    for k in range(1, tables):
        cold = cold + pooled_in[k - 1]
    feat_ref[:, :width] = cold.astype(jnp.bfloat16)


def hand_out(feat_ref, grad_ref, feat_out, grad_out, sems):
    copies = [
        pltpu.make_async_copy(feat_ref, feat_out, sems.at[0]),
        pltpu.make_async_copy(grad_ref, grad_out, sems.at[1]),
    ]
    for copy in copies:
        copy.start()
    for copy in copies:
        copy.wait()


def shards(
    tables,
    blks,
    cold_table,
    slot_row,
    slot_sample,
    slot_count,
    hot_table,
    hot_index,
    hot_count,
    hot_cotangent,
):
    slots = slot_row.shape[1]
    req_rows = slots // LANES
    samples, width = hot_cotangent.shape
    hot_rows = hot_table.shape[0]
    zs = blks // 2
    block = hot_rows // blks
    share = block // tables
    f32 = jnp.float32
    dma = pltpu.SemaphoreType.DMA
    vmem = pl.BlockSpec(memory_space=pltpu.VMEM)
    features, hot_grad = pl.pallas_call(
        functools.partial(kernel, tables, blks),
        out_shape=(
            jax.ShapeDtypeStruct((samples, 2 * width), jnp.bfloat16),
            jax.ShapeDtypeStruct((block, width), f32),
        ),
        in_specs=[pl.BlockSpec(memory_space=pl.ANY)] + [vmem] * 7,
        out_specs=(vmem, vmem),
        scratch_shapes=[
            pltpu.VMEM(cold_table.shape, jnp.bfloat16),
            pltpu.VMEM(cold_table.shape, f32),
            pltpu.VMEM((tables, 3, req_rows, LANES), jnp.int32),
            pltpu.VMEM((tables - 1, 3, req_rows, LANES), jnp.int32),
            pltpu.SMEM((tables, req_rows, LANES), jnp.int32),
            pltpu.VMEM((hot_rows, samples), jnp.bfloat16),
            pltpu.VMEM((2, zs, block, width), f32),
            pltpu.VMEM((zs, block, width), f32),
            pltpu.VMEM((tables, zs, share, width), f32),
            pltpu.VMEM((tables - 1, zs, share, width), f32),
            pltpu.VMEM((zs, share, width), f32),
            pltpu.VMEM((zs - 1, share, width), f32),
            pltpu.VMEM((req_rows, LANES, width), f32),
            pltpu.VMEM((samples, slots), jnp.bfloat16),
            pltpu.VMEM((tables - 1, samples, width), f32),
            pltpu.VMEM((tables - 1, samples, width), f32),
            pltpu.VMEM((share, width), f32),
            pltpu.VMEM((tables - 1, share, width), f32),
            dma((2 * (samples // LANES),)),
            dma((tables,)),
            dma((tables - 1,)),
            dma((tables - 1,)),
            dma((2,)),
            dma((tables - 1,)),
            dma((tables - 1,)),
            dma((zs - 1,)),
            dma((zs - 1,)),
            dma((tables - 1,)),
            dma((tables - 1,)),
            dma((tables - 1,)),
            dma((tables - 1,)),
        ],
        compiler_params=pltpu.CompilerParams(
            collective_id=0, has_side_effects=True, vmem_limit_bytes=56 * 1024 * 1024
        ),
    )(
        cold_table,
        slot_row,
        slot_sample,
        slot_count,
        hot_table,
        hot_index.T,
        hot_count.T,
        hot_cotangent,
    )
    features, hot_grad = pl.pallas_call(
        hand_out,
        out_shape=(
            jax.ShapeDtypeStruct(features.shape, features.dtype),
            jax.ShapeDtypeStruct(hot_grad.shape, hot_grad.dtype),
        ),
        in_specs=[pl.BlockSpec(memory_space=pl.ANY)] * 2,
        out_specs=(vmem, vmem),
        scratch_shapes=[dma((2,))],
    )(features, hot_grad)
    return features, hot_grad


def solution(mesh):
    both = P(("table", "blk"), None)
    return jax.shard_map(
        functools.partial(shards, mesh.shape["table"], mesh.shape["blk"]),
        mesh=mesh,
        in_specs=(P("table", None), both, both, both, P(), both, both, both),
        out_specs=(both, P("blk", None)),
        check_vma=False,
    )
```

```python
import functools

import jax
import jax.numpy as jnp
from jax import lax
from jax.experimental import pallas as pl
from jax.experimental.pallas import tpu as pltpu
from jax.sharding import PartitionSpec as P

MESH = pl.DeviceIdType.MESH
cold_scale = 0.03125
hot_scale = 0.0625
code_limit = 32767.0
LANES = 128
AHEAD = 24
PIECE = 16


def encode(values):
    top = jnp.maximum(jnp.max(jnp.abs(values), axis=0, keepdims=True), 1e-30)
    codes = jnp.round(values * (code_limit / top)).astype(jnp.int32).astype(jnp.int16)
    return codes, jnp.broadcast_to(top * (1.0 / code_limit), (8, values.shape[1]))


def decode(codes, step):
    return codes.astype(jnp.int32).astype(jnp.float32) * step[0:1]


def kernel(
    tables,
    blks,
    table_hbm,
    row_ref,
    sample_ref,
    slot_count_ref,
    hot_ref,
    index_ref,
    count_ref,
    cot_ref,
    feat_ref,
    grad_ref,
    staged,
    wide,
    req_ref,
    req_in,
    rows_smem,
    inc,
    grad_all,
    core_in,
    halves,
    half_codes,
    half_steps,
    table_in,
    table_steps,
    quarter,
    z_in,
    gathered,
    weights,
    pooled,
    pooled_steps,
    pooled_in,
    pooled_in_steps,
    total,
    shares,
    stage_sem,
    smem_sem,
    req_send,
    req_recv,
    core_sem,
    tab_send,
    tab_recv,
    tab_step_send,
    tab_step_recv,
    z_send,
    z_recv,
    ag_send,
    ag_recv,
    pool_send,
    pool_recv,
    pool_step_send,
    pool_step_recv,
):
    me_t = lax.axis_index("table")
    me_b = lax.axis_index("blk")
    core = lax.rem(me_b, 2)
    me_z = me_b // 2
    zs = blks // 2
    samples = cot_ref.shape[0]
    hot_rows = hot_ref.shape[0]
    block = hot_rows // blks
    share = block // tables
    req_rows = req_ref.shape[2]
    width = hot_ref.shape[1]
    chunks = stage_sem.shape[0]
    chunk = table_hbm.shape[0] // chunks

    stage_copies = []
    for i in range(chunks):
        part = pl.ds(i * chunk, chunk)
        copy = pltpu.make_async_copy(table_hbm.at[part], staged.at[part], stage_sem.at[i])
        copy.start()
        stage_copies.append(copy)

    def table_peer(k):
        return (me_t ^ k, me_b)

    def z_peer(k):
        return (me_t, lax.rem(me_z + k, zs) * 2 + core)

    core_peer = (me_t, me_z * 2 + 1 - core)
    partners = [table_peer(k) for k in range(1, tables)]
    partners += [z_peer(k) for k in range(1, zs)] + [core_peer]
    barrier = pltpu.get_barrier_semaphore()
    for partner in partners:
        pl.semaphore_signal(barrier, inc=1, device_id=partner, device_id_type=MESH)
    for f, ref in enumerate((row_ref, sample_ref, slot_count_ref)):
        for peer in range(tables):
            for i in range(req_rows):
                req_ref[peer, f, i : i + 1, :] = ref[peer : peer + 1, i * LANES : (i + 1) * LANES]
    pl.semaphore_wait(barrier, len(partners))

    def send(src, dst, send_sem, recv_sem, to):
        copy = pltpu.make_async_remote_copy(
            src_ref=src,
            dst_ref=dst,
            send_sem=send_sem,
            recv_sem=recv_sem,
            device_id=to,
            device_id_type=MESH,
        )
        copy.start()
        return copy

    req_copies = [
        send(
            req_ref.at[me_t ^ k],
            req_in.at[k - 1],
            req_send.at[k - 1],
            req_recv.at[k - 1],
            table_peer(k),
        )
        for k in range(1, tables)
    ]

    tile = 64
    for lane in range(samples // LANES):
        cols = pl.ds(lane * LANES, LANES)
        lookups = index_ref.shape[0]
        idx = [index_ref[k : k + 1, cols] for k in range(lookups)]
        wts = [count_ref[k : k + 1, cols].astype(jnp.float32) * hot_scale for k in range(lookups)]
        ids = lax.broadcasted_iota(jnp.int32, (tile, LANES), 0)

        per_chunk = hot_rows // tile // 2
        wide_rows = chunk // per_chunk
        for half in range(2):
            c = lane * 2 + half
            stage_copies[c].wait()

            def add_tile(r, carry):
                base = pl.multiple_of((half * per_chunk + r) * tile, tile)
                part = pl.ds(pl.multiple_of(c * chunk + r * wide_rows, wide_rows), wide_rows)
                wide[part, :] = staged[part, :].astype(jnp.float32)
                here = ids + base
                acc = jnp.where(here == idx[0], wts[0], 0.0)
                for k in range(1, lookups):
                    acc = acc + jnp.where(here == idx[k], wts[k], 0.0)
                inc[pl.ds(base, tile), cols] = acc.astype(jnp.bfloat16)
                return carry

            lax.fori_loop(0, per_chunk, add_tile, 0)

    def grad_block(b, carry):
        base = pl.multiple_of(b * block, block)
        grad_all[lax.rem(b, 2), b // 2] = jnp.dot(
            inc[pl.ds(base, block), :], cot_ref[...], preferred_element_type=jnp.float32
        )
        return carry

    lax.fori_loop(0, blks, grad_block, 0)
    core_copy = send(grad_all.at[1 - core], core_in, core_sem.at[0], core_sem.at[1], core_peer)

    own_copy = pltpu.make_async_copy(req_ref.at[me_t, 0], rows_smem.at[tables - 1], smem_sem.at[tables - 1])
    own_copy.start()
    smem_copies = []
    for k in range(1, tables):
        req_copies[k - 1].wait()
        copy = pltpu.make_async_copy(req_in.at[k - 1, 0], rows_smem.at[k - 1], smem_sem.at[k - 1])
        copy.start()
        smem_copies.append(copy)
    smem_copies.append(own_copy)

    for copy in smem_copies:
        copy.wait()

    def pool(slot, load_meta):
        def body(i, carry):
            base = pl.multiple_of(i * LANES, LANES)
            sample = load_meta(1, i)
            weight = load_meta(2, i).astype(jnp.float32) * cold_scale
            sample = jnp.broadcast_to(sample, (8, LANES))
            weight = jnp.broadcast_to(weight, (8, LANES))
            ids = lax.broadcasted_iota(jnp.int32, (8, LANES), 0)
            pieces = samples // PIECE
            got, done = [], 0
            for j in range(LANES + AHEAD):
                if j < LANES:
                    got.append(wide[pl.ds(rows_smem[slot, i, j], 1), :])
                if j >= AHEAD:
                    at = j - AHEAD
                    gathered[i, at : at + 1, :] = got[at]
                while j < LANES and done < (j + 1) * pieces // LANES:
                    first = done * PIECE
                    piece = [
                        jnp.where(ids + (first + r) == sample, weight, 0.0)
                        for r in range(0, PIECE, 8)
                    ]
                    weights[first : first + PIECE, pl.ds(base, LANES)] = jnp.concatenate(
                        piece, axis=0
                    ).astype(jnp.bfloat16)
                    done += 1
            return carry

        lax.fori_loop(0, req_rows, body, 0)
        picked = gathered[...].reshape(req_rows * LANES, width).astype(jnp.bfloat16)
        return jnp.dot(weights[...], picked, preferred_element_type=jnp.float32)

    def pool_peer(k):
        sums = pool(k - 1, lambda f, i: req_in[k - 1, f, pl.ds(i, 1), :])
        pooled[k - 1], pooled_steps[k - 1] = encode(sums)
        return [
            send(
                pooled_steps.at[k - 1],
                pooled_in_steps.at[k - 1],
                pool_step_send.at[k - 1],
                pool_step_recv.at[k - 1],
                table_peer(k),
            ),
            send(
                pooled.at[k - 1],
                pooled_in.at[k - 1],
                pool_send.at[k - 1],
                pool_recv.at[k - 1],
                table_peer(k),
            ),
        ]

    def core_stage():
        core_copy.wait()
        for part in range(tables):
            rows = pl.ds(part * share, share)
            half = grad_all[core, :, rows, :] + core_in[:, rows, :]
            halves[part] = half
            half_codes[part], half_steps[part] = encode(half.reshape(zs * share, width))
        copies = []
        for k in range(1, tables):
            copies.append(
                send(
                    half_steps.at[me_t ^ k],
                    table_steps.at[k - 1],
                    tab_step_send.at[k - 1],
                    tab_step_recv.at[k - 1],
                    table_peer(k),
                )
            )
            copies.append(
                send(
                    half_codes.at[me_t ^ k],
                    table_in.at[k - 1],
                    tab_send.at[k - 1],
                    tab_recv.at[k - 1],
                    table_peer(k),
                )
            )
        return copies

    def table_stage(copies):
        for copy in copies:
            copy.wait()
        acc = halves[me_t]
        for k in range(1, tables):
            acc = acc + decode(table_in[k - 1], table_steps[k - 1]).reshape(zs, share, width)
        quarter[...] = acc
        return [
            send(
                quarter.at[lax.rem(me_z + k, zs)],
                z_in.at[k - 1],
                z_send.at[k - 1],
                z_recv.at[k - 1],
                z_peer(k),
            )
            for k in range(1, zs)
        ]

    def z_stage(copies):
        for copy in copies:
            copy.wait()
        acc = quarter[me_z]
        for k in range(1, zs):
            acc = acc + z_in[k - 1]
        total[...] = acc
        return [
            send(total, shares.at[k - 1], ag_send.at[k - 1], ag_recv.at[k - 1], table_peer(k))
            for k in range(1, tables)
        ]

    def gather_stage(copies):
        for copy in copies:
            copy.wait()
        grad_ref[pl.ds(pl.multiple_of(me_t * share, share), share), :] = total[...]
        for k in range(1, tables):
            source = me_t ^ k
            grad_ref[pl.ds(pl.multiple_of(source * share, share), share), :] = shares[k - 1]

    pool_copies = []
    state = core_stage()
    stages = [table_stage, z_stage, gather_stage]
    for n, k in enumerate(reversed(range(1, tables))):
        pool_copies.append(pool_peer(k))
        if n < len(stages):
            state = stages[n](state)
    cold = pool(tables - 1, lambda f, i: req_ref[me_t, f, pl.ds(i, 1), :])
    hot_t = lax.dot_general(
        hot_ref[...], inc[...], (((0,), (0,)), ((), ())), preferred_element_type=jnp.float32
    )
    feat_ref[:, width:] = hot_t.T.astype(jnp.bfloat16)
    for copies in pool_copies:
        for copy in copies:
            copy.wait()
    for k in range(1, tables):
        cold = cold + decode(pooled_in[k - 1], pooled_in_steps[k - 1])
    feat_ref[:, :width] = cold.astype(jnp.bfloat16)


def hand_out(feat_ref, grad_ref, feat_out, grad_out, sems):
    copies = [
        pltpu.make_async_copy(feat_ref, feat_out, sems.at[0]),
        pltpu.make_async_copy(grad_ref, grad_out, sems.at[1]),
    ]
    for copy in copies:
        copy.start()
    for copy in copies:
        copy.wait()


def shards(
    tables,
    blks,
    cold_table,
    slot_row,
    slot_sample,
    slot_count,
    hot_table,
    hot_index,
    hot_count,
    hot_cotangent,
):
    slots = slot_row.shape[1]
    req_rows = slots // LANES
    samples, width = hot_cotangent.shape
    hot_rows = hot_table.shape[0]
    zs = blks // 2
    block = hot_rows // blks
    share = block // tables
    f32 = jnp.float32
    dma = pltpu.SemaphoreType.DMA
    vmem = pl.BlockSpec(memory_space=pltpu.VMEM)
    features, hot_grad = pl.pallas_call(
        functools.partial(kernel, tables, blks),
        out_shape=(
            jax.ShapeDtypeStruct((samples, 2 * width), jnp.bfloat16),
            jax.ShapeDtypeStruct((block, width), f32),
        ),
        in_specs=[pl.BlockSpec(memory_space=pl.ANY)] + [vmem] * 7,
        out_specs=(vmem, vmem),
        scratch_shapes=[
            pltpu.VMEM(cold_table.shape, jnp.bfloat16),
            pltpu.VMEM(cold_table.shape, f32),
            pltpu.VMEM((tables, 3, req_rows, LANES), jnp.int32),
            pltpu.VMEM((tables - 1, 3, req_rows, LANES), jnp.int32),
            pltpu.SMEM((tables, req_rows, LANES), jnp.int32),
            pltpu.VMEM((hot_rows, samples), jnp.bfloat16),
            pltpu.VMEM((2, zs, block, width), f32),
            pltpu.VMEM((zs, block, width), f32),
            pltpu.VMEM((tables, zs, share, width), f32),
            pltpu.VMEM((tables, zs * share, width), jnp.int16),
            pltpu.VMEM((tables, 8, width), f32),
            pltpu.VMEM((tables - 1, zs * share, width), jnp.int16),
            pltpu.VMEM((tables - 1, 8, width), f32),
            pltpu.VMEM((zs, share, width), f32),
            pltpu.VMEM((zs - 1, share, width), f32),
            pltpu.VMEM((req_rows, LANES, width), f32),
            pltpu.VMEM((samples, slots), jnp.bfloat16),
            pltpu.VMEM((tables - 1, samples, width), jnp.int16),
            pltpu.VMEM((tables - 1, 8, width), f32),
            pltpu.VMEM((tables - 1, samples, width), jnp.int16),
            pltpu.VMEM((tables - 1, 8, width), f32),
            pltpu.VMEM((share, width), f32),
            pltpu.VMEM((tables - 1, share, width), f32),
            dma((2 * (samples // LANES),)),
            dma((tables,)),
            dma((tables - 1,)),
            dma((tables - 1,)),
            dma((2,)),
            dma((tables - 1,)),
            dma((tables - 1,)),
            dma((tables - 1,)),
            dma((tables - 1,)),
            dma((zs - 1,)),
            dma((zs - 1,)),
            dma((tables - 1,)),
            dma((tables - 1,)),
            dma((tables - 1,)),
            dma((tables - 1,)),
            dma((tables - 1,)),
            dma((tables - 1,)),
        ],
        compiler_params=pltpu.CompilerParams(
            collective_id=0, has_side_effects=True, vmem_limit_bytes=56 * 1024 * 1024
        ),
    )(
        cold_table,
        slot_row,
        slot_sample,
        slot_count,
        hot_table,
        hot_index.T,
        hot_count.T,
        hot_cotangent,
    )
    features, hot_grad = pl.pallas_call(
        hand_out,
        out_shape=(
            jax.ShapeDtypeStruct(features.shape, features.dtype),
            jax.ShapeDtypeStruct(hot_grad.shape, hot_grad.dtype),
        ),
        in_specs=[pl.BlockSpec(memory_space=pl.ANY)] * 2,
        out_specs=(vmem, vmem),
        scratch_shapes=[dma((2,))],
    )(features, hot_grad)
    return features, hot_grad


def solution(mesh):
    both = P(("table", "blk"), None)
    return jax.shard_map(
        functools.partial(shards, mesh.shape["table"], mesh.shape["blk"]),
        mesh=mesh,
        in_specs=(P("table", None), both, both, both, P(), both, both, both),
        out_specs=(both, P("blk", None)),
        check_vma=False,
    )
```

```python
import functools

import jax
import jax.numpy as jnp
from jax import lax
from jax.experimental import pallas as pl
from jax.experimental.pallas import tpu as pltpu
from jax.sharding import PartitionSpec as P

MESH = pl.DeviceIdType.MESH
cold_scale = 0.03125
hot_scale = 0.0625
code_limit = 32767.0
LANES = 128
AHEAD = 24
PIECE = 16


def encode(values):
    top = jnp.maximum(jnp.max(jnp.abs(values), axis=0, keepdims=True), 1e-30)
    codes = jnp.round(values * (code_limit / top)).astype(jnp.int32).astype(jnp.int16)
    return codes, jnp.broadcast_to(top * (1.0 / code_limit), (8, values.shape[1]))


def decode(codes, step):
    return codes.astype(jnp.int32).astype(jnp.float32) * step[0:1]


def kernel(
    tables,
    blks,
    loads,
    table_hbm,
    row_ref,
    sample_ref,
    slot_count_ref,
    hot_ref,
    index_ref,
    count_ref,
    cot_ref,
    feat_ref,
    grad_ref,
    staged,
    wide,
    req_ref,
    req_in,
    rows_smem,
    inc,
    grad_all,
    core_in,
    halves,
    half_codes,
    half_steps,
    table_in,
    table_steps,
    quarter,
    z_in,
    gathered,
    weights,
    pooled,
    pooled_steps,
    pooled_in,
    pooled_in_steps,
    total,
    shares,
    stage_sem,
    smem_sem,
    req_send,
    req_recv,
    core_sem,
    tab_send,
    tab_recv,
    tab_step_send,
    tab_step_recv,
    z_send,
    z_recv,
    ag_send,
    ag_recv,
    pool_send,
    pool_recv,
    pool_step_send,
    pool_step_recv,
):
    me_t = lax.axis_index("table")
    me_b = lax.axis_index("blk")
    core = lax.rem(me_b, 2)
    me_z = me_b // 2
    zs = blks // 2
    samples = cot_ref.shape[0]
    hot_rows = hot_ref.shape[0]
    block = hot_rows // blks
    share = block // tables
    req_rows = req_ref.shape[2]
    width = hot_ref.shape[1]
    chunks = stage_sem.shape[0]
    chunk = table_hbm.shape[0] // chunks

    stage_copies = []
    for i in range(chunks):
        part = pl.ds(i * chunk, chunk)
        copy = pltpu.make_async_copy(table_hbm.at[part], staged.at[part], stage_sem.at[i])
        copy.start()
        stage_copies.append(copy)

    def table_peer(k):
        return (me_t ^ k, me_b)

    def z_peer(k):
        return (me_t, lax.rem(me_z + k, zs) * 2 + core)

    core_peer = (me_t, me_z * 2 + 1 - core)
    partners = [table_peer(k) for k in range(1, tables)]
    partners += [z_peer(k) for k in range(1, zs)] + [core_peer]
    barrier = pltpu.get_barrier_semaphore()
    for partner in partners:
        pl.semaphore_signal(barrier, inc=1, device_id=partner, device_id_type=MESH)
    for copy in loads:
        copy.wait()
    for f, ref in enumerate((row_ref, sample_ref, slot_count_ref)):
        for peer in range(tables):
            for i in range(req_rows):
                req_ref[peer, f, i : i + 1, :] = ref[peer : peer + 1, i * LANES : (i + 1) * LANES]

    def send(src, dst, send_sem, recv_sem, to):
        copy = pltpu.make_async_remote_copy(
            src_ref=src,
            dst_ref=dst,
            send_sem=send_sem,
            recv_sem=recv_sem,
            device_id=to,
            device_id_type=MESH,
        )
        copy.start()
        return copy

    tile = 64
    none = jnp.zeros((PIECE, LANES), jnp.bfloat16)

    def spread(row):
        return jnp.broadcast_to(row, (PIECE, LANES))

    for lane in range(samples // LANES):
        cols = pl.ds(lane * LANES, LANES)
        lookups = index_ref.shape[0]
        idx = [spread(index_ref[k : k + 1, cols]).astype(jnp.int16) for k in range(lookups)]
        wts = [
            spread(count_ref[k : k + 1, cols].astype(jnp.float32) * hot_scale).astype(jnp.bfloat16)
            for k in range(lookups)
        ]
        ids = lax.broadcasted_iota(jnp.int32, (PIECE, LANES), 0)

        per_chunk = hot_rows // tile // 2
        wide_rows = chunk // per_chunk
        for half in range(2):
            c = lane * 2 + half
            stage_copies[c].wait()

            def add_tile(r, carry):
                base = pl.multiple_of((half * per_chunk + r) * tile, tile)
                part = pl.ds(pl.multiple_of(c * chunk + r * wide_rows, wide_rows), wide_rows)
                wide[part, :] = staged[part, :].astype(jnp.float32)
                for p in range(0, tile, PIECE):
                    here = (ids + (base + p)).astype(jnp.int16)
                    acc = jnp.where(here == idx[0], wts[0], none)
                    for k in range(1, lookups):
                        acc = acc + jnp.where(here == idx[k], wts[k], none)
                    inc[pl.ds(base + p, PIECE), cols] = acc
                return carry

            lax.fori_loop(0, per_chunk, add_tile, 0)

        if lane == 0:
            pl.semaphore_wait(barrier, len(partners))
            req_copies = [
                send(
                    req_ref.at[me_t ^ k],
                    req_in.at[k - 1],
                    req_send.at[k - 1],
                    req_recv.at[k - 1],
                    table_peer(k),
                )
                for k in range(1, tables)
            ]

    def grad_block(b, carry):
        base = pl.multiple_of(b * block, block)
        grad_all[lax.rem(b, 2), b // 2] = jnp.dot(
            inc[pl.ds(base, block), :], cot_ref[...], preferred_element_type=jnp.float32
        )
        return carry

    lax.fori_loop(0, blks, grad_block, 0)
    core_copy = send(grad_all.at[1 - core], core_in, core_sem.at[0], core_sem.at[1], core_peer)

    own_copy = pltpu.make_async_copy(req_ref.at[me_t, 0], rows_smem.at[tables - 1], smem_sem.at[tables - 1])
    own_copy.start()
    smem_copies = []
    for k in range(1, tables):
        req_copies[k - 1].wait()
        copy = pltpu.make_async_copy(req_in.at[k - 1, 0], rows_smem.at[k - 1], smem_sem.at[k - 1])
        copy.start()
        smem_copies.append(copy)
    smem_copies.append(own_copy)

    for copy in smem_copies:
        copy.wait()

    def pool(slot, load_meta):
        def body(i, carry):
            base = pl.multiple_of(i * LANES, LANES)
            sample = load_meta(1, i)
            weight = load_meta(2, i).astype(jnp.float32) * cold_scale
            sample = spread(sample).astype(jnp.int16)
            weight = spread(weight).astype(jnp.bfloat16)
            ids = lax.broadcasted_iota(jnp.int32, (PIECE, LANES), 0)
            pieces = samples // PIECE
            got, done = [], 0
            for j in range(LANES + AHEAD):
                if j < LANES:
                    got.append(wide[pl.ds(rows_smem[slot, i, j], 1), :])
                if j >= AHEAD:
                    at = j - AHEAD
                    gathered[i, at : at + 1, :] = got[at]
                while j < LANES and done < (j + 1) * pieces // LANES:
                    first = done * PIECE
                    here = (ids + first).astype(jnp.int16)
                    weights[first : first + PIECE, pl.ds(base, LANES)] = jnp.where(
                        here == sample, weight, none
                    )
                    done += 1
            return carry

        lax.fori_loop(0, req_rows, body, 0)
        picked = gathered[...].reshape(req_rows * LANES, width).astype(jnp.bfloat16)
        return jnp.dot(weights[...], picked, preferred_element_type=jnp.float32)

    def pool_peer(k):
        sums = pool(k - 1, lambda f, i: req_in[k - 1, f, pl.ds(i, 1), :])
        pooled[k - 1], pooled_steps[k - 1] = encode(sums)
        return [
            send(
                pooled_steps.at[k - 1],
                pooled_in_steps.at[k - 1],
                pool_step_send.at[k - 1],
                pool_step_recv.at[k - 1],
                table_peer(k),
            ),
            send(
                pooled.at[k - 1],
                pooled_in.at[k - 1],
                pool_send.at[k - 1],
                pool_recv.at[k - 1],
                table_peer(k),
            ),
        ]

    def core_stage():
        core_copy.wait()
        for part in range(tables):
            rows = pl.ds(part * share, share)
            half = grad_all[core, :, rows, :] + core_in[:, rows, :]
            halves[part] = half
            half_codes[part], half_steps[part] = encode(half.reshape(zs * share, width))
        copies = []
        for k in range(1, tables):
            copies.append(
                send(
                    half_steps.at[me_t ^ k],
                    table_steps.at[k - 1],
                    tab_step_send.at[k - 1],
                    tab_step_recv.at[k - 1],
                    table_peer(k),
                )
            )
            copies.append(
                send(
                    half_codes.at[me_t ^ k],
                    table_in.at[k - 1],
                    tab_send.at[k - 1],
                    tab_recv.at[k - 1],
                    table_peer(k),
                )
            )
        return copies

    def table_stage(copies):
        for copy in copies:
            copy.wait()
        acc = halves[me_t]
        for k in range(1, tables):
            acc = acc + decode(table_in[k - 1], table_steps[k - 1]).reshape(zs, share, width)
        quarter[...] = acc
        return [
            send(
                quarter.at[lax.rem(me_z + k, zs)],
                z_in.at[k - 1],
                z_send.at[k - 1],
                z_recv.at[k - 1],
                z_peer(k),
            )
            for k in range(1, zs)
        ]

    def z_stage(copies):
        for copy in copies:
            copy.wait()
        acc = quarter[me_z]
        for k in range(1, zs):
            acc = acc + z_in[k - 1]
        total[...] = acc
        return [
            send(total, shares.at[k - 1], ag_send.at[k - 1], ag_recv.at[k - 1], table_peer(k))
            for k in range(1, tables)
        ]

    def gather_stage(copies):
        for copy in copies:
            copy.wait()
        grad_ref[pl.ds(pl.multiple_of(me_t * share, share), share), :] = total[...]
        for k in range(1, tables):
            source = me_t ^ k
            grad_ref[pl.ds(pl.multiple_of(source * share, share), share), :] = shares[k - 1]

    pool_copies = []
    state = core_stage()
    stages = [table_stage, z_stage, gather_stage]
    for n, k in enumerate(reversed(range(1, tables))):
        pool_copies.append(pool_peer(k))
        if n < len(stages):
            state = stages[n](state)
    cold = pool(tables - 1, lambda f, i: req_ref[me_t, f, pl.ds(i, 1), :])
    hot_t = lax.dot_general(
        hot_ref[...], inc[...], (((0,), (0,)), ((), ())), preferred_element_type=jnp.float32
    )
    feat_ref[:, width:] = hot_t.T.astype(jnp.bfloat16)
    for copies in pool_copies:
        for copy in copies:
            copy.wait()
    for k in range(1, tables):
        cold = cold + decode(pooled_in[k - 1], pooled_in_steps[k - 1])
    feat_ref[:, :width] = cold.astype(jnp.bfloat16)


def load_first(tables, blks, table_hbm, *refs):
    sources, outs, held, sem, rest = refs[:7], refs[7:9], refs[9:16], refs[16], refs[17:]
    loads = [
        pltpu.make_async_copy(source, ref, sem.at[i])
        for i, (source, ref) in enumerate(zip(sources, held))
    ]
    for copy in loads:
        copy.start()
    kernel(tables, blks, loads, table_hbm, *held, *outs, *rest)


def hand_out(feat_ref, grad_ref, feat_out, grad_out, sems):
    copies = [
        pltpu.make_async_copy(feat_ref, feat_out, sems.at[0]),
        pltpu.make_async_copy(grad_ref, grad_out, sems.at[1]),
    ]
    for copy in copies:
        copy.start()
    for copy in copies:
        copy.wait()


def shards(
    tables,
    blks,
    cold_table,
    slot_row,
    slot_sample,
    slot_count,
    hot_table,
    hot_index,
    hot_count,
    hot_cotangent,
):
    slots = slot_row.shape[1]
    req_rows = slots // LANES
    samples, width = hot_cotangent.shape
    hot_rows = hot_table.shape[0]
    zs = blks // 2
    block = hot_rows // blks
    share = block // tables
    f32 = jnp.float32
    dma = pltpu.SemaphoreType.DMA
    vmem = pl.BlockSpec(memory_space=pltpu.VMEM)
    operands = (
        slot_row,
        slot_sample,
        slot_count,
        hot_table,
        hot_index.T,
        hot_count.T,
        hot_cotangent,
    )
    features, hot_grad = pl.pallas_call(
        functools.partial(load_first, tables, blks),
        out_shape=(
            jax.ShapeDtypeStruct((samples, 2 * width), jnp.bfloat16),
            jax.ShapeDtypeStruct((block, width), f32),
        ),
        in_specs=[pl.BlockSpec(memory_space=pltpu.HBM)] * 8,
        out_specs=(vmem, vmem),
        scratch_shapes=[
            *[pltpu.VMEM(a.shape, a.dtype) for a in operands],
            dma((7,)),
            pltpu.VMEM(cold_table.shape, jnp.bfloat16),
            pltpu.VMEM(cold_table.shape, f32),
            pltpu.VMEM((tables, 3, req_rows, LANES), jnp.int32),
            pltpu.VMEM((tables - 1, 3, req_rows, LANES), jnp.int32),
            pltpu.SMEM((tables, req_rows, LANES), jnp.int32),
            pltpu.VMEM((hot_rows, samples), jnp.bfloat16),
            pltpu.VMEM((2, zs, block, width), f32),
            pltpu.VMEM((zs, block, width), f32),
            pltpu.VMEM((tables, zs, share, width), f32),
            pltpu.VMEM((tables, zs * share, width), jnp.int16),
            pltpu.VMEM((tables, 8, width), f32),
            pltpu.VMEM((tables - 1, zs * share, width), jnp.int16),
            pltpu.VMEM((tables - 1, 8, width), f32),
            pltpu.VMEM((zs, share, width), f32),
            pltpu.VMEM((zs - 1, share, width), f32),
            pltpu.VMEM((req_rows, LANES, width), f32),
            pltpu.VMEM((samples, slots), jnp.bfloat16),
            pltpu.VMEM((tables - 1, samples, width), jnp.int16),
            pltpu.VMEM((tables - 1, 8, width), f32),
            pltpu.VMEM((tables - 1, samples, width), jnp.int16),
            pltpu.VMEM((tables - 1, 8, width), f32),
            pltpu.VMEM((share, width), f32),
            pltpu.VMEM((tables - 1, share, width), f32),
            dma((2 * (samples // LANES),)),
            dma((tables,)),
            dma((tables - 1,)),
            dma((tables - 1,)),
            dma((2,)),
            dma((tables - 1,)),
            dma((tables - 1,)),
            dma((tables - 1,)),
            dma((tables - 1,)),
            dma((zs - 1,)),
            dma((zs - 1,)),
            dma((tables - 1,)),
            dma((tables - 1,)),
            dma((tables - 1,)),
            dma((tables - 1,)),
            dma((tables - 1,)),
            dma((tables - 1,)),
        ],
        compiler_params=pltpu.CompilerParams(
            collective_id=0, has_side_effects=True, vmem_limit_bytes=56 * 1024 * 1024
        ),
    )(cold_table, *operands)
    features, hot_grad = pl.pallas_call(
        hand_out,
        out_shape=(
            jax.ShapeDtypeStruct(features.shape, features.dtype),
            jax.ShapeDtypeStruct(hot_grad.shape, hot_grad.dtype),
        ),
        in_specs=[pl.BlockSpec(memory_space=pl.ANY)] * 2,
        out_specs=(vmem, vmem),
        scratch_shapes=[dma((2,))],
    )(features, hot_grad)
    return features, hot_grad


def solution(mesh):
    both = P(("table", "blk"), None)
    return jax.shard_map(
        functools.partial(shards, mesh.shape["table"], mesh.shape["blk"]),
        mesh=mesh,
        in_specs=(P("table", None), both, both, both, P(), both, both, both),
        out_specs=(both, P("blk", None)),
        check_vma=False,
    )
```

```python
import functools

import jax
import jax.numpy as jnp
from jax import lax
from jax.experimental import pallas as pl
from jax.experimental.pallas import tpu as pltpu
from jax.sharding import PartitionSpec as P

MESH = pl.DeviceIdType.MESH
cold_scale = 0.03125
hot_scale = 0.0625
code_limit = 32767.0
LANES = 128
AHEAD = 12
PIECE = 16


def encode(values):
    top = jnp.maximum(jnp.max(jnp.abs(values), axis=0, keepdims=True), 1e-30)
    codes = jnp.round(values * (code_limit / top)).astype(jnp.int32).astype(jnp.int16)
    return codes, jnp.broadcast_to(top * (1.0 / code_limit), (8, values.shape[1]))


def decode(codes, step):
    return codes.astype(jnp.int32).astype(jnp.float32) * step[0:1]


def kernel(
    tables,
    blks,
    loads,
    table_hbm,
    row_ref,
    sample_ref,
    slot_count_ref,
    hot_ref,
    index_ref,
    count_ref,
    cot_ref,
    feat_ref,
    grad_ref,
    staged,
    wide,
    req_ref,
    req_in,
    rows_smem,
    inc,
    grad_all,
    core_in,
    halves,
    half_codes,
    half_steps,
    table_in,
    table_steps,
    quarter,
    z_in,
    gathered,
    weights,
    pooled,
    pooled_steps,
    pooled_in,
    pooled_in_steps,
    total,
    shares,
    stage_sem,
    smem_sem,
    req_send,
    req_recv,
    core_sem,
    tab_send,
    tab_recv,
    tab_step_send,
    tab_step_recv,
    z_send,
    z_recv,
    ag_send,
    ag_recv,
    pool_send,
    pool_recv,
    pool_step_send,
    pool_step_recv,
):
    me_t = lax.axis_index("table")
    me_b = lax.axis_index("blk")
    core = lax.rem(me_b, 2)
    me_z = me_b // 2
    zs = blks // 2
    samples = cot_ref.shape[0]
    hot_rows = hot_ref.shape[0]
    block = hot_rows // blks
    share = block // tables
    req_rows = req_ref.shape[2]
    width = hot_ref.shape[1]
    chunks = stage_sem.shape[0]
    chunk = table_hbm.shape[0] // chunks

    stage_copies = []
    for i in range(chunks):
        part = pl.ds(i * chunk, chunk)
        copy = pltpu.make_async_copy(table_hbm.at[part], staged.at[part], stage_sem.at[i])
        copy.start()
        stage_copies.append(copy)

    def table_peer(k):
        return (me_t ^ k, me_b)

    def z_peer(k):
        return (me_t, lax.rem(me_z + k, zs) * 2 + core)

    core_peer = (me_t, me_z * 2 + 1 - core)
    partners = [table_peer(k) for k in range(1, tables)]
    partners += [z_peer(k) for k in range(1, zs)] + [core_peer]
    barrier = pltpu.get_barrier_semaphore()
    for partner in partners:
        pl.semaphore_signal(barrier, inc=1, device_id=partner, device_id_type=MESH)
    for copy in loads:
        copy.wait()
    for f, ref in enumerate((row_ref, sample_ref, slot_count_ref)):
        for peer in range(tables):
            for i in range(req_rows):
                req_ref[peer, f, i : i + 1, :] = ref[peer : peer + 1, i * LANES : (i + 1) * LANES]

    def send(src, dst, send_sem, recv_sem, to):
        copy = pltpu.make_async_remote_copy(
            src_ref=src,
            dst_ref=dst,
            send_sem=send_sem,
            recv_sem=recv_sem,
            device_id=to,
            device_id_type=MESH,
        )
        copy.start()
        return copy

    tile = 64
    none = jnp.zeros((PIECE, LANES), jnp.bfloat16)

    def spread(row):
        return jnp.broadcast_to(row, (PIECE, LANES))

    for lane in range(samples // LANES):
        cols = pl.ds(lane * LANES, LANES)
        lookups = index_ref.shape[0]
        idx = [spread(index_ref[k : k + 1, cols]).astype(jnp.int16) for k in range(lookups)]
        wts = [
            spread(count_ref[k : k + 1, cols].astype(jnp.float32) * hot_scale).astype(jnp.bfloat16)
            for k in range(lookups)
        ]
        ids = lax.broadcasted_iota(jnp.int32, (PIECE, LANES), 0)

        per_chunk = hot_rows // tile // 2
        wide_rows = chunk // per_chunk
        for half in range(2):
            c = lane * 2 + half
            stage_copies[c].wait()

            def add_tile(r, carry):
                base = pl.multiple_of((half * per_chunk + r) * tile, tile)
                part = pl.ds(pl.multiple_of(c * chunk + r * wide_rows, wide_rows), wide_rows)
                wide[part, :] = staged[part, :].astype(jnp.float32)
                for p in range(0, tile, PIECE):
                    here = (ids + (base + p)).astype(jnp.int16)
                    acc = jnp.where(here == idx[0], wts[0], none)
                    for k in range(1, lookups):
                        acc = acc + jnp.where(here == idx[k], wts[k], none)
                    inc[pl.ds(base + p, PIECE), cols] = acc
                return carry

            lax.fori_loop(0, per_chunk, add_tile, 0)

        if lane == 0:
            pl.semaphore_wait(barrier, len(partners))
            req_copies = [
                send(
                    req_ref.at[me_t ^ k],
                    req_in.at[k - 1],
                    req_send.at[k - 1],
                    req_recv.at[k - 1],
                    table_peer(k),
                )
                for k in range(1, tables)
            ]

    def grad_block(b, carry):
        base = pl.multiple_of(b * block, block)
        grad_all[lax.rem(b, 2), b // 2] = jnp.dot(
            inc[pl.ds(base, block), :], cot_ref[...], preferred_element_type=jnp.float32
        )
        return carry

    lax.fori_loop(0, blks, grad_block, 0)
    core_copy = send(grad_all.at[1 - core], core_in, core_sem.at[0], core_sem.at[1], core_peer)

    own_copy = pltpu.make_async_copy(req_ref.at[me_t, 0], rows_smem.at[tables - 1], smem_sem.at[tables - 1])
    own_copy.start()
    smem_copies = []
    for k in range(1, tables):
        req_copies[k - 1].wait()
        copy = pltpu.make_async_copy(req_in.at[k - 1, 0], rows_smem.at[k - 1], smem_sem.at[k - 1])
        copy.start()
        smem_copies.append(copy)
    smem_copies.append(own_copy)

    for copy in smem_copies:
        copy.wait()

    def pool(slot, load_meta):
        def body(i, carry):
            base = pl.multiple_of(i * LANES, LANES)
            sample = load_meta(1, i)
            weight = load_meta(2, i).astype(jnp.float32) * cold_scale
            sample = spread(sample).astype(jnp.int16)
            weight = spread(weight).astype(jnp.bfloat16)
            ids = lax.broadcasted_iota(jnp.int32, (PIECE, LANES), 0)
            pieces = samples // PIECE
            got, done = [], 0
            for j in range(LANES + AHEAD):
                if j < LANES:
                    got.append(wide[pl.ds(rows_smem[slot, i, j], 1), :])
                if j >= AHEAD:
                    at = j - AHEAD
                    gathered[i, at : at + 1, :] = got[at]
                while j < LANES and done < (j + 1) * pieces // LANES:
                    first = done * PIECE
                    here = (ids + first).astype(jnp.int16)
                    weights[first : first + PIECE, pl.ds(base, LANES)] = jnp.where(
                        here == sample, weight, none
                    )
                    done += 1
            return carry

        lax.fori_loop(0, req_rows, body, 0)
        picked = gathered[...].reshape(req_rows * LANES, width).astype(jnp.bfloat16)
        return jnp.dot(weights[...], picked, preferred_element_type=jnp.float32)

    def pool_peer(k):
        sums = pool(k - 1, lambda f, i: req_in[k - 1, f, pl.ds(i, 1), :])
        pooled[k - 1], pooled_steps[k - 1] = encode(sums)
        return [
            send(
                pooled_steps.at[k - 1],
                pooled_in_steps.at[k - 1],
                pool_step_send.at[k - 1],
                pool_step_recv.at[k - 1],
                table_peer(k),
            ),
            send(
                pooled.at[k - 1],
                pooled_in.at[k - 1],
                pool_send.at[k - 1],
                pool_recv.at[k - 1],
                table_peer(k),
            ),
        ]

    def core_stage():
        core_copy.wait()
        for part in range(tables):
            rows = pl.ds(part * share, share)
            half = grad_all[core, :, rows, :] + core_in[:, rows, :]
            halves[part] = half
            half_codes[part], half_steps[part] = encode(half.reshape(zs * share, width))
        copies = []
        for k in range(1, tables):
            copies.append(
                send(
                    half_steps.at[me_t ^ k],
                    table_steps.at[k - 1],
                    tab_step_send.at[k - 1],
                    tab_step_recv.at[k - 1],
                    table_peer(k),
                )
            )
            copies.append(
                send(
                    half_codes.at[me_t ^ k],
                    table_in.at[k - 1],
                    tab_send.at[k - 1],
                    tab_recv.at[k - 1],
                    table_peer(k),
                )
            )
        return copies

    def table_stage(copies):
        for copy in copies:
            copy.wait()
        acc = halves[me_t]
        for k in range(1, tables):
            acc = acc + decode(table_in[k - 1], table_steps[k - 1]).reshape(zs, share, width)
        quarter[...] = acc
        return [
            send(
                quarter.at[lax.rem(me_z + k, zs)],
                z_in.at[k - 1],
                z_send.at[k - 1],
                z_recv.at[k - 1],
                z_peer(k),
            )
            for k in range(1, zs)
        ]

    def z_stage(copies):
        for copy in copies:
            copy.wait()
        acc = quarter[me_z]
        for k in range(1, zs):
            acc = acc + z_in[k - 1]
        total[...] = acc
        return [
            send(total, shares.at[k - 1], ag_send.at[k - 1], ag_recv.at[k - 1], table_peer(k))
            for k in range(1, tables)
        ]

    def gather_stage(copies):
        for copy in copies:
            copy.wait()
        grad_ref[pl.ds(pl.multiple_of(me_t * share, share), share), :] = total[...]
        for k in range(1, tables):
            source = me_t ^ k
            grad_ref[pl.ds(pl.multiple_of(source * share, share), share), :] = shares[k - 1]

    pool_copies = []
    state = core_stage()
    stages = [table_stage, z_stage, gather_stage]
    for n, k in enumerate(reversed(range(1, tables))):
        pool_copies.append(pool_peer(k))
        if n < len(stages):
            state = stages[n](state)
    cold = pool(tables - 1, lambda f, i: req_ref[me_t, f, pl.ds(i, 1), :])
    hot_t = lax.dot_general(
        hot_ref[...], inc[...], (((0,), (0,)), ((), ())), preferred_element_type=jnp.float32
    )
    feat_ref[:, width:] = hot_t.T.astype(jnp.bfloat16)
    for copies in pool_copies:
        for copy in copies:
            copy.wait()
    for k in range(1, tables):
        cold = cold + decode(pooled_in[k - 1], pooled_in_steps[k - 1])
    feat_ref[:, :width] = cold.astype(jnp.bfloat16)


def load_first(tables, blks, table_hbm, *refs):
    sources, outs, held, sem, rest = refs[:7], refs[7:9], refs[9:16], refs[16], refs[17:]
    loads = [
        pltpu.make_async_copy(source, ref, sem.at[i])
        for i, (source, ref) in enumerate(zip(sources, held))
    ]
    for copy in loads:
        copy.start()
    kernel(tables, blks, loads, table_hbm, *held, *outs, *rest)


def hand_out(feat_ref, grad_ref, feat_out, grad_out, sems):
    copies = [
        pltpu.make_async_copy(feat_ref, feat_out, sems.at[0]),
        pltpu.make_async_copy(grad_ref, grad_out, sems.at[1]),
    ]
    for copy in copies:
        copy.start()
    for copy in copies:
        copy.wait()


def shards(
    tables,
    blks,
    cold_table,
    slot_row,
    slot_sample,
    slot_count,
    hot_table,
    hot_index,
    hot_count,
    hot_cotangent,
):
    slots = slot_row.shape[1]
    req_rows = slots // LANES
    samples, width = hot_cotangent.shape
    hot_rows = hot_table.shape[0]
    zs = blks // 2
    block = hot_rows // blks
    share = block // tables
    f32 = jnp.float32
    dma = pltpu.SemaphoreType.DMA
    vmem = pl.BlockSpec(memory_space=pltpu.VMEM)
    operands = (
        slot_row,
        slot_sample,
        slot_count,
        hot_table,
        hot_index.T,
        hot_count.T,
        hot_cotangent,
    )
    features, hot_grad = pl.pallas_call(
        functools.partial(load_first, tables, blks),
        out_shape=(
            jax.ShapeDtypeStruct((samples, 2 * width), jnp.bfloat16),
            jax.ShapeDtypeStruct((block, width), f32),
        ),
        in_specs=[pl.BlockSpec(memory_space=pltpu.HBM)] * 8,
        out_specs=(vmem, vmem),
        scratch_shapes=[
            *[pltpu.VMEM(a.shape, a.dtype) for a in operands],
            dma((7,)),
            pltpu.VMEM(cold_table.shape, jnp.bfloat16),
            pltpu.VMEM(cold_table.shape, f32),
            pltpu.VMEM((tables, 3, req_rows, LANES), jnp.int32),
            pltpu.VMEM((tables - 1, 3, req_rows, LANES), jnp.int32),
            pltpu.SMEM((tables, req_rows, LANES), jnp.int32),
            pltpu.VMEM((hot_rows, samples), jnp.bfloat16),
            pltpu.VMEM((2, zs, block, width), f32),
            pltpu.VMEM((zs, block, width), f32),
            pltpu.VMEM((tables, zs, share, width), f32),
            pltpu.VMEM((tables, zs * share, width), jnp.int16),
            pltpu.VMEM((tables, 8, width), f32),
            pltpu.VMEM((tables - 1, zs * share, width), jnp.int16),
            pltpu.VMEM((tables - 1, 8, width), f32),
            pltpu.VMEM((zs, share, width), f32),
            pltpu.VMEM((zs - 1, share, width), f32),
            pltpu.VMEM((req_rows, LANES, width), f32),
            pltpu.VMEM((samples, slots), jnp.bfloat16),
            pltpu.VMEM((tables - 1, samples, width), jnp.int16),
            pltpu.VMEM((tables - 1, 8, width), f32),
            pltpu.VMEM((tables - 1, samples, width), jnp.int16),
            pltpu.VMEM((tables - 1, 8, width), f32),
            pltpu.VMEM((share, width), f32),
            pltpu.VMEM((tables - 1, share, width), f32),
            dma((2 * (samples // LANES),)),
            dma((tables,)),
            dma((tables - 1,)),
            dma((tables - 1,)),
            dma((2,)),
            dma((tables - 1,)),
            dma((tables - 1,)),
            dma((tables - 1,)),
            dma((tables - 1,)),
            dma((zs - 1,)),
            dma((zs - 1,)),
            dma((tables - 1,)),
            dma((tables - 1,)),
            dma((tables - 1,)),
            dma((tables - 1,)),
            dma((tables - 1,)),
            dma((tables - 1,)),
        ],
        compiler_params=pltpu.CompilerParams(
            collective_id=0, has_side_effects=True, vmem_limit_bytes=56 * 1024 * 1024
        ),
    )(cold_table, *operands)
    features, hot_grad = pl.pallas_call(
        hand_out,
        out_shape=(
            jax.ShapeDtypeStruct(features.shape, features.dtype),
            jax.ShapeDtypeStruct(hot_grad.shape, hot_grad.dtype),
        ),
        in_specs=[pl.BlockSpec(memory_space=pl.ANY)] * 2,
        out_specs=(vmem, vmem),
        scratch_shapes=[dma((2,))],
    )(features, hot_grad)
    return features, hot_grad


def solution(mesh):
    both = P(("table", "blk"), None)
    return jax.shard_map(
        functools.partial(shards, mesh.shape["table"], mesh.shape["blk"]),
        mesh=mesh,
        in_specs=(P("table", None), both, both, both, P(), both, both, both),
        out_specs=(both, P("blk", None)),
        check_vma=False,
    )
```
